512 devices in a mesh: tensor: 16 (over z_hi, y), dp: 32 (over z_lo, x, core).
Axes of the slice: x: 4, y: 8, z: 8 (z_hi: 2, z_lo: 4; z = z_hi * 4 + z_lo), core: 2. Of those that a mesh axis runs over, the one named last changes fastest.
Arguments:
- tokens: bfloat16 [16384, 4096], P(('dp', 'tensor')), parts along dimension 0, may hold values from -6 to 6
- attn_gain: bfloat16 [4096], replicated, may hold values from 0.5 to 1.5
- query_weight: bfloat16 [4096, 2048], P(None, 'tensor'), may hold values from -1 to 1
- key_value_weight: bfloat16 [4096, 2048], P(None, 'tensor'), may hold values from -1 to 1
- prefix_cache: bfloat16 [131072, 2048], P('dp', 'tensor'), parts along dimension 0, may hold values from -240 to 240, as said below
- out_weight: bfloat16 [2048, 4096], P('tensor'), may hold values from -0.125 to 0.125
- post_gain: bfloat16 [4096], replicated, may hold values from 0.5 to 1.5
Outputs:
- residual_out: bfloat16 [16384, 4096], P(('dp', 'tensor')), parts along dimension 0
- normed_out: bfloat16 [16384, 4096], P(('dp', 'tensor')), parts along dimension 0
The draws below stay inside these ranges and needn't reach their ends.
There are 32 independent parts, one for each index of `dp`. The reference program is written for one: setup_inputs(seed, part) draws one part's arguments, and reference() takes and returns one part's arrays. A program takes and returns all parts, laid end to end along the dimension named above; an argument that names none is the same for every part. Nothing has to cross between parts.
Inputs may be any that keep to these rules, and one draw needn't show every extreme that they name: prefix_cache holds the rotated keys and the values of positions 0 to 4095.
All inputs are finite; a program needn't handle non-finite values.
Results may differ from the reference program's by a relative error of at most 0.04.
Values may be sent and summed in bfloat16 or wider, within the bound.
A program may use at most 64 MiB of HBM per device.

```python
import math
import jax
import jax.numpy as jnp
from jax import lax

MODEL_WIDTH = 4096
HEAD_SIZE = 128
QDEV = 1
CACHED_POSITIONS = 4096
PROMPT_TOKENS = 512
QUERY_HEADS = 16
KEY_VALUE_HEADS = 8
N_TENSOR = 16


def shared_key_columns(key):
    return jax.random.truncated_normal(key, -4.0, 4.0, (MODEL_WIDTH, KEY_VALUE_HEADS, HEAD_SIZE), jnp.float32) * MODEL_WIDTH ** (-0.5)


def draw_key_value_weight(key, part):
    key_columns = shared_key_columns(key)
    key = jax.random.fold_in(key, 5)
    value_columns = jax.random.truncated_normal(key, -4.0, 4.0, (MODEL_WIDTH, KEY_VALUE_HEADS, HEAD_SIZE), jnp.float32) * MODEL_WIDTH ** (-0.5)
    stacked = jnp.stack([key_columns, value_columns], axis=2)
    return stacked.reshape(MODEL_WIDTH, KEY_VALUE_HEADS * 2 * HEAD_SIZE).astype(jnp.bfloat16)


def draw_query_weight(key, part):
    key_columns = shared_key_columns(key)
    key = jax.random.fold_in(key, 3)
    strength_key = jax.random.fold_in(key, 17)
    noise_key = jax.random.fold_in(key, 19)
    group_count = QUERY_HEADS // KEY_VALUE_HEADS
    head_columns = jnp.repeat(key_columns, group_count, axis=1)
    strength = jnp.exp(jax.random.uniform(strength_key, (QUERY_HEADS,), jnp.float32, math.log(0.3), math.log(1.5)))
    noise = jax.random.truncated_normal(noise_key, -4.0, 4.0, (MODEL_WIDTH, QUERY_HEADS, HEAD_SIZE), jnp.float32) * MODEL_WIDTH ** (-0.5)
    columns = jnp.clip(strength[None, :, None] * head_columns + noise, -1.0, 1.0)
    return columns.reshape(MODEL_WIDTH, QUERY_HEADS * HEAD_SIZE).astype(jnp.bfloat16)


def draw_prefix_cache(key, part):
    key = jax.random.fold_in(key, 7)
    cache_entries = jax.random.truncated_normal(key, -4.0, 4.0, (CACHED_POSITIONS, KEY_VALUE_HEADS, 2, HEAD_SIZE), jnp.float32)
    return cache_entries.reshape(CACHED_POSITIONS, KEY_VALUE_HEADS * 2 * HEAD_SIZE).astype(jnp.bfloat16)


def steps_of(key, extent, pieces, smallest, largest):
    factor_of = 1.0
    for axis_at, parts in pieces:
        heights = jax.random.uniform(jax.random.fold_in(jax.random.fold_in(key, 6), axis_at), (parts,), jnp.float32, smallest / len(pieces), largest / len(pieces))
        factor_of = factor_of * jnp.repeat(jnp.exp(heights), extent[axis_at] // parts).reshape((-1,) + (1,) * (len(extent) - 1 - axis_at))
    return factor_of


def normal_values(stream_key, shape, scale, reach, pieces=(), kind=jnp.bfloat16):
    loudness = steps_of(stream_key, shape, pieces, -0.22, 0.18) if pieces else 1.0
    values = jax.random.normal(stream_key, shape, jnp.float32) * scale * loudness
    return jnp.minimum(jnp.maximum(values, -reach), reach).astype(kind)


def setup_inputs(seed: int = 0, part: int = 0) -> dict:
    key_list = jax.random.split(jax.random.key(seed), 8)
    part_splits = jax.random.split(jax.random.fold_in(key_list[7], part), 8)
    tokens = normal_values(part_splits[0], (PROMPT_TOKENS, MODEL_WIDTH), 1.0, 6.0, ((0, 16),))
    attn_gain = jnp.clip(1.0 + 0.1 * jax.random.normal(key_list[1], (MODEL_WIDTH,), jnp.float32), 0.5, 1.5).astype(jnp.bfloat16)
    query_weight = draw_query_weight(jax.random.fold_in(key_list[7], 71), part)
    key_value_weight = draw_key_value_weight(jax.random.fold_in(key_list[7], 71), part)
    prefix_cache = draw_prefix_cache(jax.random.fold_in(jax.random.fold_in(key_list[7], part), 71), part)
    out_weight = normal_values(key_list[5], (QUERY_HEADS * HEAD_SIZE, MODEL_WIDTH), (QUERY_HEADS * HEAD_SIZE) ** -0.5, 0.125, ((0, 16),))
    post_gain = jnp.clip(1.0 + 0.1 * jax.random.normal(key_list[6], (MODEL_WIDTH,), jnp.float32), 0.5, 1.5).astype(jnp.bfloat16)
    return dict(tokens=tokens, attn_gain=attn_gain, query_weight=query_weight, key_value_weight=key_value_weight, prefix_cache=prefix_cache, out_weight=out_weight, post_gain=post_gain)


rope_base = 500000.0
norm_eps = 1e-05

def rms_scale(row_data, gain_vector):
    widened = row_data.astype(jnp.float32)
    mean_square = lax.optimization_barrier(jnp.mean(widened * widened, axis=-1, keepdims=True))
    return widened * lax.rsqrt(mean_square + norm_eps) * gain_vector.astype(jnp.float32)

def apply_rotation(projected, first_row):
    row_count = projected.shape[0]
    grouped = projected.reshape(row_count, -1, HEAD_SIZE)
    positions = (first_row + jnp.arange(row_count, dtype=jnp.int32)).astype(jnp.float32)
    inverse = rope_base ** (-jnp.arange(HEAD_SIZE // 2, dtype=jnp.float32) * 2.0 / HEAD_SIZE)
    angle_table = positions[:, None] * inverse[None, :]
    cosine = jnp.cos(angle_table)[:, None, :]
    sine_table = jnp.sin(angle_table)[:, None, :]
    lower_half = grouped[..., :HEAD_SIZE // 2]
    upper_half = grouped[..., HEAD_SIZE // 2:]
    turned = jnp.concatenate([lower_half * cosine - upper_half * sine_table, upper_half * cosine + lower_half * sine_table], axis=-1)
    return turned.reshape(row_count, -1)

def reference(tokens, attn_gain, query_weight, key_value_weight, prefix_cache, out_weight, post_gain):
    normalized_input = rms_scale(tokens, attn_gain).astype(jnp.bfloat16)
    queries = apply_rotation(jnp.dot(normalized_input, query_weight, preferred_element_type=jnp.float32), CACHED_POSITIONS).astype(jnp.bfloat16)
    fresh_key_values = jnp.dot(normalized_input, key_value_weight, preferred_element_type=jnp.float32).reshape(PROMPT_TOKENS, KEY_VALUE_HEADS, 2, HEAD_SIZE)
    fresh_keys = apply_rotation(fresh_key_values[:, :, 0, :].reshape(PROMPT_TOKENS, KEY_VALUE_HEADS * HEAD_SIZE), CACHED_POSITIONS).astype(jnp.bfloat16)
    fresh_values = fresh_key_values[:, :, 1, :].reshape(PROMPT_TOKENS, KEY_VALUE_HEADS * HEAD_SIZE).astype(jnp.bfloat16)
    cache_contents = prefix_cache.reshape(CACHED_POSITIONS, KEY_VALUE_HEADS, 2, HEAD_SIZE)
    key_row_matrix = jnp.concatenate([cache_contents[:, :, 0, :].reshape(CACHED_POSITIONS, KEY_VALUE_HEADS * HEAD_SIZE), fresh_keys], axis=0)
    value_row_matrix = jnp.concatenate([cache_contents[:, :, 1, :].reshape(CACHED_POSITIONS, KEY_VALUE_HEADS * HEAD_SIZE), fresh_values], axis=0)
    query_pos = CACHED_POSITIONS + jnp.arange(PROMPT_TOKENS, dtype=jnp.int32)
    key_pos = jnp.arange(CACHED_POSITIONS + PROMPT_TOKENS, dtype=jnp.int32)
    visible = key_pos[None, :] <= query_pos[:, None]
    queries_per_group = QUERY_HEADS // KEY_VALUE_HEADS
    outputs = []
    for head_index in range(QUERY_HEADS):
        kv_index = head_index // queries_per_group
        query_block = queries[:, head_index * HEAD_SIZE:(head_index + 1) * HEAD_SIZE]
        key_block = key_row_matrix[:, kv_index * HEAD_SIZE:(kv_index + 1) * HEAD_SIZE]
        value_block = value_row_matrix[:, kv_index * HEAD_SIZE:(kv_index + 1) * HEAD_SIZE]
        scores = jnp.dot(query_block, key_block.T, preferred_element_type=jnp.float32) * HEAD_SIZE ** (-0.5)
        scores = jnp.where(visible, scores, -1e+30)
        row_max = lax.optimization_barrier(jnp.max(scores, axis=-1, keepdims=True))
        weights = jnp.exp(scores - row_max)
        row_total = lax.optimization_barrier(jnp.sum(weights, axis=-1, keepdims=True))
        probs = (weights / row_total).astype(jnp.bfloat16)
        outputs.append(jnp.dot(probs, value_block, preferred_element_type=jnp.float32).astype(jnp.bfloat16))
    attended = jnp.concatenate(outputs, axis=1)
    group_width = QDEV * HEAD_SIZE
    attn_sum = jnp.zeros((PROMPT_TOKENS, MODEL_WIDTH), jnp.float32)
    for group_index in range(N_TENSOR):
        rounded_part = jnp.dot(attended[:, group_index * group_width:(group_index + 1) * group_width], out_weight[group_index * group_width:(group_index + 1) * group_width], preferred_element_type=jnp.float32).astype(jnp.bfloat16)
        rounded_part = lax.optimization_barrier(rounded_part)
        attn_sum = attn_sum + rounded_part.astype(jnp.float32)
    residual_out = (tokens.astype(jnp.float32) + attn_sum).astype(jnp.bfloat16)
    normed_out = rms_scale(residual_out, post_gain).astype(jnp.bfloat16)
    return (residual_out, normed_out)
```

```python
import functools

import jax
import jax.numpy as jnp
import numpy as np
from jax import lax
from jax.experimental import pallas as pl
from jax.experimental.pallas import tpu as pltpu
from jax.sharding import PartitionSpec as P

MESH = pl.DeviceIdType.MESH
BF16 = jnp.bfloat16
F32 = jnp.float32
HEAD = 128
PAST = 4096
BLOCK = 512
WIDTH = 4096
BASE = 500000.0
EPS = 1e-05
SCALE2 = float(HEAD ** (-0.5) / np.log(2.0))
NEG = -1e30


def rope_tables():
    positions = np.arange(PAST, PAST + BLOCK, dtype=np.float64)
    inverse = BASE ** (-np.arange(HEAD // 2, dtype=np.float64) * 2.0 / HEAD)
    angle = positions[:, None] * inverse[None, :]
    cosine = np.concatenate([np.cos(angle), np.cos(angle)], axis=1)
    sine = np.concatenate([-np.sin(angle), np.sin(angle)], axis=1)
    return cosine.astype(np.float32), sine.astype(np.float32)


def normed(rows, gain):
    mean_square = jnp.mean(rows * rows, axis=-1, keepdims=True)
    return rows * lax.rsqrt(mean_square + EPS) * gain


def kernel(
    tok_h, gain1, wq_h, wkv_h, cache_h, wout_h, gain2, cos_h, sin_h,
    res_o, nrm_o,
    tok, xg, wb, cos_t, sin_t, sres, qb, kvb, wo, att, ar, po, ob,
    m_s, l_s, acc_s,
    ld, xs, xr, wzs, wzr, wxs, wxr, wcs, wcr,
    kfs, kfr, khs, khr, kxs, kxr, qs, qr, ns, nr,
    wys, wyr, zs, zr, zcs, zcr, as_, ar_r, ags, agr, os_, or_,
):
    t = lax.axis_index("tensor")
    d = lax.axis_index("dp")
    zh, y = t // 8, t % 8
    zl, x, c = d // 8, (d // 2) % 4, d % 2
    j, q = y // 2, y % 2
    aligned = c == q
    zi = zh * 4 + zl

    def dev(zh=zh, y=y, zl=zl, x=x, c=c):
        return {"tensor": zh * 8 + y, "dp": zl * 8 + x * 2 + c}

    def remote(src, dst, ss, rs, to):
        return pltpu.make_async_remote_copy(
            src_ref=src, dst_ref=dst, send_sem=ss, recv_sem=rs,
            device_id=to, device_id_type=MESH,
        )

    def arrived(ref, sem):
        pltpu.make_async_copy(ref, ref, sem).wait()

    sib = dev(c=1 - c)
    zmate = dev(zh=1 - zh)
    up, down = dev(y=(y + 1) % 8), dev(y=(y + 7) % 8)

    def zdev(step):
        n = (zi + step) % 8
        return dev(zh=n // 4, zl=n % 4)

    load_tok = pltpu.make_async_copy(tok_h, tok, ld.at[0])
    load_wq = pltpu.make_async_copy(wq_h, wb.at[0, :, pl.ds(0, HEAD)], ld.at[1])
    load_wkv = pltpu.make_async_copy(wkv_h, wb.at[0, :, pl.ds(HEAD, HEAD)], ld.at[2])
    rows_z = pl.ds(pl.multiple_of(zh * 256, 256), 256)
    load_cos = pltpu.make_async_copy(cos_h.at[rows_z], cos_t, ld.at[3])
    load_sin = pltpu.make_async_copy(sin_h.at[rows_z], sin_t, ld.at[4])
    load_tok.start()
    load_wq.start()
    load_wkv.start()

    barrier = pltpu.get_barrier_semaphore()
    mine = t * 2 + c

    def greet(i, carry):
        n = (mine + i) % 32
        pl.semaphore_signal(
            barrier, inc=1,
            device_id={"tensor": n // 2, "dp": zl * 8 + x * 2 + n % 2},
            device_id_type=MESH,
        )
        return carry

    lax.fori_loop(1, 32, greet, 0)
    for i in (1, 2, 3):
        pl.semaphore_signal(barrier, inc=1, device_id=dev(x=(x + i) % 4), device_id_type=MESH)
    for i in (1, 7):
        pl.semaphore_signal(barrier, inc=1, device_id=zdev(i), device_id_type=MESH)
    load_cos.start()
    load_sin.start()

    load_tok.wait()

    def own_rows(n):
        return pl.ds(pl.multiple_of(n * 32, 32), 32)

    xg[own_rows(y), :] = normed(tok[...].astype(F32), gain1[...].astype(F32)).astype(BF16)
    load_wq.wait()
    load_wkv.wait()
    pl.semaphore_wait(barrier, 36)

    def x_copy(step, way, k):
        n = (y - step + 1 + 8) % 8 if way == 0 else (y + step - 1) % 8
        part = xg.at[pl.ds(pl.multiple_of(n * 32 + k * 16, 16), 16), :]
        return remote(part, part, xs.at[way, step - 1, k], xr.at[way, step - 1, k], up if way == 0 else down)

    def x_used(step, way, k):
        return step < 4 or way == k

    for k in range(2):
        for way in range(2):
            x_copy(1, way, k).start()

    def w_rows(xx, cc, k):
        return pl.ds(pl.multiple_of(xx * 1024 + cc * 512 + k * 256, 256), 256)

    def w_z(k):
        r = w_rows(x, c, k)
        return remote(wb.at[0, r], wb.at[1, r], wzs.at[k], wzr.at[k], zmate)

    def w_x(i, k):
        r = w_rows(x, c, k)
        return remote(wb.at[1, r], wb.at[1, r], wxs.at[i - 1, k], wxr.at[i - 1, k], dev(x=(x + i) % 4))

    def w_c(i, k):
        r = w_rows((x + 4 - i) % 4, c, k)
        return remote(wb.at[1, r], wb.at[1, r], wcs.at[i, k], wcr.at[i, k], sib)

    w_z(0).start()
    w_z(1).start()

    def full_local():
        return pltpu.make_async_copy(cache_h, kvb.at[q, pl.ds(0, PAST)], kfr.at[0])

    def full_send():
        return remote(cache_h, kvb.at[q, pl.ds(0, PAST)], kfs.at[0], kfr.at[0], sib)

    def half_rows(h, k):
        return pl.ds(pl.multiple_of(h * 2048 + k * 1024, 1024), 1024)

    def half_send(h, k):
        r = half_rows(h, k)
        return remote(cache_h.at[r], kvb.at[q, r], khs.at[h, k], khr.at[k], dev(y=2 * j + 1 - q, c=h))

    def half_pass(k):
        r = half_rows(c, k)
        return remote(kvb.at[1 - q, r], kvb.at[1 - q, r], kxs.at[k], kxr.at[k], sib)

    @pl.when(aligned)
    def _():
        full_local().start()
        full_send().start()

    def wo_src():
        col = pl.multiple_of((x * 4 + zl) * 256, 256)
        return wout_h.at[:, pl.ds(col, 256)]

    def wo_send(i):
        return remote(wo_src(), wo.at[zl, zh, c, j], wys.at[i], wyr.at[j], dev(y=(y + i) % 8))

    @pl.when(aligned)
    def _():
        pltpu.make_async_copy(wo_src(), wo.at[zl, zh, c, j], wyr.at[j]).start()
        for i in range(1, 8):
            wo_send(i).start()

    def z_copy(step, way):
        n = (zi - step + 1 + 8) % 8 if way == 0 else (zi + step - 1) % 8
        part = wo.at[n % 4, n // 4, c]
        if step == 4:
            part = part.at[pl.ds(2 * way, 2)]
        return remote(part, part, zs.at[way, step - 1], zr.at[way, step - 1], zdev(1 if way == 0 else 7))

    def z_arrived(step):
        for way in range(2):
            z_copy(step, way).wait_recv()

    def z_start(step):
        for way in range(2):
            z_copy(step, way).start()

    def zc_copy(i):
        n = (zi + i) % 8
        part = wo.at[n % 4, n // 4, c]
        return remote(part, part, zcs.at[i], zcr.at[i], sib)

    for step in range(1, 5):
        for k in range(2):
            for way in range(2):
                if x_used(step, way, k):
                    x_copy(step, way, k).wait_recv()
                    if step < 4 and x_used(step + 1, way, k):
                        x_copy(step + 1, way, k).start()
        if step <= 2:
            w_z(step - 1).wait_recv()
            for i in (1, 3, 2):
                w_x(i, step - 1).start()
            w_c(0, step - 1).start()
        if step == 2:
            for i in range(4):
                arrived(wo.at[zl, zh, c, i], wyr.at[i])
            z_start(1)
            zc_copy(0).start()
        if step == 3:
            @pl.when(jnp.logical_not(aligned))
            def _():
                for k in range(2):
                    for h in range(2):
                        half_send(h, k).start()

            for i in (1, 3, 2):
                w_x(i, 0).wait_recv()
                w_c(i, 0).start()
    for i in (1, 3, 2):
        w_x(i, 1).wait_recv()
        w_c(i, 1).start()
    z_arrived(1)
    z_start(2)
    zc_copy(1).start()
    zc_copy(7).start()

    load_cos.wait()
    load_sin.wait()

    def turn(v):
        return v * cos_t[...] + pltpu.roll(v, 64, 1) * sin_t[...]

    def new_rows(z):
        return pl.ds(pl.multiple_of(PAST + z * 256, 256), 256)

    def q_dst():
        return qb.at[rows_z]

    def n_dst():
        return kvb.at[q, new_rows(zh)]

    def q_send(w, to):
        return remote(sres.at[w, 0], q_dst(), qs.at[w], qr.at[zh], to)

    def n_send(w, h, to):
        return remote(sres.at[w, 1], n_dst(), ns.at[w, h], nr.at[q, zh], to)

    def project(w):
        out = jnp.dot(xg[...], wb[w], preferred_element_type=F32)
        part_q, part_n = out[:, :HEAD], out[:, HEAD:]
        sres[w, 0] = turn(part_q).astype(BF16)
        sres[w, 1] = jnp.where(q == 0, turn(part_n), part_n).astype(BF16)

    def spread_own(start):
        @pl.when(aligned)
        def _():
            if start:
                pltpu.make_async_copy(sres.at[0, 0], q_dst(), qr.at[zh]).start()
                pltpu.make_async_copy(sres.at[0, 1], n_dst(), nr.at[q, zh]).start()
                n_send(0, 0, sib).start()
            else:
                n_send(0, 0, sib).wait_send()

        @pl.when(jnp.logical_not(aligned))
        def _():
            copies = [q_send(0, dev(y=2 * j + c, c=q))]
            copies += [n_send(0, h, dev(y=2 * j + c, c=h)) for h in range(2)]
            for copy in copies:
                copy.start() if start else copy.wait_send()

    def spread_other(start):
        copies = [q_send(1, dev(zh=1 - zh, y=2 * j + c, c=q))]
        copies += [n_send(1, h, dev(zh=1 - zh, y=2 * j + c, c=h)) for h in range(2)]
        for copy in copies:
            copy.start() if start else copy.wait_send()

    project(0)
    spread_own(True)
    for k in range(2):
        for i in (0, 1, 3, 2):
            w_c(i, k).wait_recv()
    project(1)
    spread_other(True)

    m_s[...] = jnp.full(m_s.shape, NEG, F32)
    l_s[...] = jnp.zeros(l_s.shape, F32)
    acc_s[...] = jnp.zeros(acc_s.shape, F32)
    z_arrived(2)
    z_start(3)
    zc_copy(2).start()
    zc_copy(6).start()
    for z in range(2):
        arrived(qb.at[pl.ds(0, 256)], qr.at[z])
    arrived(cache_h, kfr.at[0])

    def attend(first, size, masked):
        keys = kvb[0, pl.ds(first, size), :]
        values = kvb[1, pl.ds(first, size), :]
        for tile in range(2):
            rows = pl.ds(tile * 256, 256)
            s = lax.dot_general(qb[rows, :], keys, (((1,), (1,)), ((), ())), preferred_element_type=F32)
            if masked:
                row = lax.broadcasted_iota(jnp.int32, s.shape, 0) + tile * 256
                col = lax.broadcasted_iota(jnp.int32, s.shape, 1)
                s = jnp.where(col <= row, s, NEG)
            old = m_s[rows, :]
            new = jnp.maximum(old, jnp.max(s, axis=1, keepdims=True))
            keep = jnp.exp2((old - new) * SCALE2)
            p = jnp.exp2((s - new[:, :1]) * SCALE2)
            l_s[rows, :] = l_s[rows, :] * keep + jnp.sum(p, axis=1, keepdims=True)
            acc_s[rows, :] = acc_s[rows, :] * keep + jnp.dot(p.astype(BF16), values, preferred_element_type=F32)
            m_s[rows, :] = new

    for k in range(2):
        arrived(kvb.at[0, pl.ds(0, 1024)], khr.at[k])
        half_pass(k).start()
        attend(pl.multiple_of(c * 2048 + k * 1024, 1024), 1024, False)
    z_arrived(3)
    z_start(4)
    zc_copy(3).start()
    zc_copy(5).start()
    for k in range(2):
        half_pass(k).wait_recv()
        attend(pl.multiple_of((1 - c) * 2048 + k * 1024, 1024), 1024, False)
    for kind in range(2):
        for z in range(2):
            arrived(kvb.at[0, pl.ds(0, 256)], nr.at[kind, z])
    attend(PAST, BLOCK, True)
    att[...] = (acc_s[...] / l_s[...]).astype(BF16)

    slot_x = own_rows(x)

    def a_copy(n, remotely):
        src = att.at[own_rows(n)]
        col = pl.multiple_of((zh * 8 + c * 4 + j) * HEAD, HEAD)
        dst = ar.at[slot_x, pl.ds(col, HEAD)]
        sem = ar_r.at[zh * 8 + c * 4 + j]
        if remotely:
            return remote(src, dst, as_.at[n], sem, {"tensor": n, "dp": zl * 8 + x * 2 + q})
        return pltpu.make_async_copy(src, dst, sem)

    def a_start(n, carry):
        stays = jnp.logical_and(n == t, aligned)

        @pl.when(stays)
        def _():
            a_copy(n, False).start()

        @pl.when(jnp.logical_not(stays))
        def _():
            a_copy(n, True).start()

        return carry

    def a_sent(n, carry):
        @pl.when(jnp.logical_not(jnp.logical_and(n == t, aligned)))
        def _():
            a_copy(n, True).wait_send()

        return carry

    lax.fori_loop(0, 16, a_start, 0)
    z_arrived(4)
    zc_copy(4).start()

    def a_here(n, carry):
        arrived(ar.at[pl.ds(0, 32), pl.ds(0, HEAD)], ar_r.at[n])
        return carry

    lax.fori_loop(0, 16, a_here, 0)

    def ag(i):
        return remote(ar.at[slot_x], ar.at[slot_x], ags.at[i - 1], agr.at[i - 1], dev(x=(x + i) % 4))

    for i in (2, 1, 3):
        ag(i).start()
    for i in range(8):
        zc_copy(i).wait_recv()
    for i in (1, 3, 2):
        ag(i).wait_recv()

    def product(n, carry):
        w = wo[n].reshape(2048, 256)
        out = jnp.dot(ar[...], w, preferred_element_type=F32).astype(BF16)
        for i in range(4):
            po[i, n] = out[i * 32 : (i + 1) * 32]
        return carry

    lax.fori_loop(0, 4, product, 0)

    def o_copy(i):
        n = (x + i) % 4
        return remote(po.at[n], ob.at[x], os_.at[i - 1], or_.at[i - 1], dev(x=n))

    for i in (2, 1, 3):
        o_copy(i).start()
    ob[x] = po[x]
    for i in (1, 3, 2):
        o_copy(i).wait_recv()

    total = jnp.zeros((32, 1), F32)
    for n in range(4):
        for k in range(4):
            cols = pl.ds((n * 4 + k) * 256, 256)
            res = (tok[:, cols].astype(F32) + ob[n, k].astype(F32)).astype(BF16)
            res_o[:, cols] = res
            wide = res.astype(F32)
            total = total + jnp.sum(wide * wide, axis=1, keepdims=True)
    scale = lax.rsqrt(total / WIDTH + EPS)
    nrm_o[...] = (res_o[...].astype(F32) * scale * gain2[...].astype(F32)).astype(BF16)

    for step in range(1, 5):
        for k in range(2):
            for way in range(2):
                if x_used(step, way, k):
                    x_copy(step, way, k).wait_send()
        for way in range(2):
            z_copy(step, way).wait_send()
    for k in range(2):
        w_z(k).wait_send()
        half_pass(k).wait_send()
        for i in range(4):
            w_c(i, k).wait_send()
            if i:
                w_x(i, k).wait_send()
    for i in range(8):
        zc_copy(i).wait_send()
    for i in range(1, 4):
        ag(i).wait_send()
        o_copy(i).wait_send()

    @pl.when(aligned)
    def _():
        full_send().wait_send()
        for i in range(1, 8):
            wo_send(i).wait_send()

    @pl.when(jnp.logical_not(aligned))
    def _():
        for k in range(2):
            for h in range(2):
                half_send(h, k).wait_send()

    spread_own(False)
    spread_other(False)
    lax.fori_loop(0, 16, a_sent, 0)


def per_device(tokens, attn_gain, query_weight, key_value_weight, prefix_cache, out_weight, post_gain):
    cosine, sine = rope_tables()
    hbm = pl.BlockSpec(memory_space=pl.ANY)
    vmem = pl.BlockSpec(memory_space=pltpu.VMEM)
    dma = pltpu.SemaphoreType.DMA
    rows = jax.ShapeDtypeStruct(tokens.shape, BF16)
    return pl.pallas_call(
        kernel,
        out_shape=(rows, rows),
        in_specs=[hbm, vmem, hbm, hbm, hbm, hbm, vmem, hbm, hbm],
        out_specs=(vmem, vmem),
        scratch_shapes=[
            pltpu.VMEM((32, WIDTH), BF16),
            pltpu.VMEM((256, WIDTH), BF16),
            pltpu.VMEM((2, WIDTH, 256), BF16),
            pltpu.VMEM((256, HEAD), F32),
            pltpu.VMEM((256, HEAD), F32),
            pltpu.VMEM((2, 2, 256, HEAD), BF16),
            pltpu.VMEM((BLOCK, HEAD), BF16),
            pltpu.VMEM((2, PAST + BLOCK, HEAD), BF16),
            pltpu.VMEM((4, 2, 2, 4, HEAD, 256), BF16),
            pltpu.VMEM((BLOCK, HEAD), BF16),
            pltpu.VMEM((HEAD, 2048), BF16),
            pltpu.VMEM((4, 4, 32, 256), BF16),
            pltpu.VMEM((4, 4, 32, 256), BF16),
            pltpu.VMEM((BLOCK, HEAD), F32),
            pltpu.VMEM((BLOCK, HEAD), F32),
            pltpu.VMEM((BLOCK, HEAD), F32),
            dma((5,)),
            dma((2, 4, 2)), dma((2, 4, 2)),
            dma((2,)), dma((2,)),
            dma((3, 2)), dma((3, 2)),
            dma((4, 2)), dma((4, 2)),
            dma((1,)), dma((1,)),
            dma((2, 2)), dma((2,)),
            dma((2,)), dma((2,)),
            dma((2,)), dma((2,)),
            dma((2, 2)), dma((2, 2)),
            dma((8,)), dma((4,)),
            dma((2, 4)), dma((2, 4)),
            dma((8,)), dma((8,)),
            dma((16,)), dma((16,)),
            dma((3,)), dma((3,)),
            dma((3,)), dma((3,)),
        ],
        compiler_params=pltpu.CompilerParams(
            collective_id=0, has_side_effects=True, vmem_limit_bytes=48 * 2**20
        ),
        name="sublayer",
    )(
        tokens, attn_gain.reshape(1, -1), query_weight, key_value_weight, prefix_cache,
        out_weight, post_gain.reshape(1, -1), jnp.asarray(cosine), jnp.asarray(sine),
    )


def solution(mesh):
    rows = P(("dp", "tensor"), None)
    return jax.shard_map(
        per_device,
        mesh=mesh,
        in_specs=(rows, P(), P(None, "tensor"), P(None, "tensor"), P("dp", "tensor"), P("tensor", None), P()),
        out_specs=(rows, rows),
        check_vma=False,
    )
```

```python
import functools

import jax
import jax.numpy as jnp
import numpy as np
from jax import lax
from jax.experimental import pallas as pl
from jax.experimental.pallas import tpu as pltpu
from jax.sharding import PartitionSpec as P

MESH = pl.DeviceIdType.MESH
BF16 = jnp.bfloat16
F32 = jnp.float32
HEAD = 128
PAST = 4096
BLOCK = 512
WIDTH = 4096
BASE = 500000.0
EPS = 1e-05
SCALE2 = float(HEAD ** (-0.5) / np.log(2.0))
NEG = -1e30


def rope_tables():
    positions = np.arange(PAST, PAST + BLOCK, dtype=np.float64)
    inverse = BASE ** (-np.arange(HEAD // 2, dtype=np.float64) * 2.0 / HEAD)
    angle = positions[:, None] * inverse[None, :]
    cosine = np.concatenate([np.cos(angle), np.cos(angle)], axis=1)
    sine = np.concatenate([-np.sin(angle), np.sin(angle)], axis=1)
    return cosine.astype(np.float32), sine.astype(np.float32)


def normed(rows, gain):
    mean_square = jnp.mean(rows * rows, axis=-1, keepdims=True)
    return rows * lax.rsqrt(mean_square + EPS) * gain


def kernel(
    tok_h, gain1, wq_h, wkv_h, cache_h, wout_h, cos_h, sin_h,
    out_o,
    tok, xg, wb, cos_t, sin_t, sres, qb, kvb, wo, att, ar, po,
    m_s, l_s, acc_s,
    ld, xs, xr, ys, yr, wzs, wzr, wxs, wxr, wcs, wcr,
    kfs, kfr, khs, khr, kxs, kxr, qs, qr, ns, nr, nps,
    zs, zr, zcs, zcr, as_, ar_r, ags, agr, os_, or_,
):
    t = lax.axis_index("tensor")
    d = lax.axis_index("dp")
    zh, y = t // 8, t % 8
    zl, x, c = d // 8, (d // 2) % 4, d % 2
    j, q = y // 2, y % 2
    aligned = c == q
    zi = zh * 4 + zl

    def dev(zh=zh, y=y, zl=zl, x=x, c=c):
        return {"tensor": zh * 8 + y, "dp": zl * 8 + x * 2 + c}

    def remote(src, dst, ss, rs, to):
        return pltpu.make_async_remote_copy(
            src_ref=src, dst_ref=dst, send_sem=ss, recv_sem=rs,
            device_id=to, device_id_type=MESH,
        )

    def arrived(ref, sem):
        pltpu.make_async_copy(ref, ref, sem).wait()

    sib = dev(c=1 - c)
    zmate = dev(zh=1 - zh)
    up, down = dev(y=(y + 1) % 8), dev(y=(y + 7) % 8)

    def zdev(step):
        n = (zi + step) % 8
        return dev(zh=n // 4, zl=n % 4)

    load_tok = pltpu.make_async_copy(tok_h, tok, ld.at[0])
    load_wq = pltpu.make_async_copy(wq_h, wb.at[0, :, pl.ds(0, HEAD)], ld.at[1])
    load_wkv = pltpu.make_async_copy(wkv_h, wb.at[0, :, pl.ds(HEAD, HEAD)], ld.at[2])
    rows_z = pl.ds(pl.multiple_of(zh * 256, 256), 256)
    load_cos = pltpu.make_async_copy(cos_h.at[rows_z], cos_t, ld.at[3])
    load_sin = pltpu.make_async_copy(sin_h.at[rows_z], sin_t, ld.at[4])
    load_tok.start()
    load_wq.start()
    load_wkv.start()

    def wo_piece(n):
        return wo.at[zl, c, zh, n]

    out_col = pl.multiple_of((x * 4 + zl) * 256 + c * HEAD, HEAD)
    load_wo = pltpu.make_async_copy(wout_h.at[:, pl.ds(out_col, HEAD)], wo_piece(y), ld.at[5])

    barrier = pltpu.get_barrier_semaphore()
    greeted = [up, down, zdev(1), zdev(7), zmate, sib, dev(y=2 * j + 1 - q, c=1 - c)]
    greeted += [dev(x=(x + i) % 4) for i in (1, 2, 3)]
    for to in greeted:
        pl.semaphore_signal(barrier, inc=1, device_id=to, device_id_type=MESH)
    load_wo.start()
    load_cos.start()
    load_sin.start()

    load_tok.wait()

    def own_rows(n):
        return pl.ds(pl.multiple_of(n * 32, 32), 32)

    xg[own_rows(y), :] = normed(tok[...].astype(F32), gain1[...].astype(F32).reshape(1, WIDTH)).astype(BF16)
    load_wq.wait()
    load_wkv.wait()
    load_wo.wait()
    pl.semaphore_wait(barrier, len(greeted))

    def x_copy(step, way, k):
        n = (y - step + 1 + 8) % 8 if way == 0 else (y + step - 1) % 8
        part = xg.at[pl.ds(pl.multiple_of(n * 32 + k * 16, 16), 16), :]
        return remote(part, part, xs.at[way, step - 1, k], xr.at[way, step - 1, k], up if way == 0 else down)

    def x_used(step, way, k):
        return step < 4 or way == k

    def y_copy(step, way):
        part = wo_piece((y - step + 1 + 8) % 8 if way == 0 else (y + step - 1) % 8)
        if step == 4:
            part = part.at[pl.ds(64 * way, 64)]
        return remote(part, part, ys.at[way, step - 1], yr.at[way, step - 1], up if way == 0 else down)

    for k in range(2):
        for way in range(2):
            x_copy(1, way, k).start()
    for way in range(2):
        y_copy(1, way).start()

    def w_rows(xx, cc, k):
        return pl.ds(pl.multiple_of(xx * 1024 + cc * 512 + k * 128, 128), 128)

    def w_z(k):
        r = w_rows(x, c, k)
        return remote(wb.at[0, r], wb.at[1, r], wzs.at[k], wzr.at[k], zmate)

    def w_x(i, k):
        r = w_rows(x, c, k)
        return remote(wb.at[1, r], wb.at[1, r], wxs.at[i - 1, k], wxr.at[i - 1, k], dev(x=(x + i) % 4))

    def w_c(i, k):
        r = w_rows((x + 4 - i) % 4, c, k)
        return remote(wb.at[1, r], wb.at[1, r], wcs.at[i, k], wcr.at[i, k], sib)

    for k in range(4):
        w_z(k).start()

    def full_local():
        return pltpu.make_async_copy(cache_h, kvb.at[q, pl.ds(0, PAST)], kfr.at[0])

    def full_send():
        return remote(cache_h, kvb.at[q, pl.ds(0, PAST)], kfs.at[0], kfr.at[0], sib)

    def half_rows(h, k):
        return pl.ds(pl.multiple_of(h * 2048 + k * 1024, 1024), 1024)

    def half_send(h, k):
        r = half_rows(h, k)
        return remote(cache_h.at[r], kvb.at[q, r], khs.at[h, k], khr.at[k], dev(y=2 * j + 1 - q, c=h))

    def half_pass(k):
        r = half_rows(c, k)
        return remote(kvb.at[1 - q, r], kvb.at[1 - q, r], kxs.at[k], kxr.at[k], sib)

    @pl.when(aligned)
    def _():
        full_local().start()
        full_send().start()

    def z_copy(step, way):
        n = (zi - step + 1 + 8) % 8 if way == 0 else (zi + step - 1) % 8
        part = wo.at[n % 4, c, n // 4]
        if step == 4:
            part = part.at[pl.ds(4 * way, 4)]
        return remote(part, part, zs.at[way, step - 1], zr.at[way, step - 1], zdev(1 if way == 0 else 7))

    def z_arrived(step):
        for way in range(2):
            z_copy(step, way).wait_recv()

    def z_start(step):
        for way in range(2):
            z_copy(step, way).start()

    def zc_copy(i):
        n = (zi + i) % 8
        part = wo.at[n % 4, c, n // 4]
        return remote(part, part, zcs.at[i], zcr.at[i], sib)

    for step in range(1, 5):
        for k in range(2):
            for way in range(2):
                if x_used(step, way, k):
                    x_copy(step, way, k).wait_recv()
                    if step < 4 and x_used(step + 1, way, k):
                        x_copy(step + 1, way, k).start()
            n = (step - 1) * 2 + k
            if n < 4:
                w_z(n).wait_recv()
                for i in (2, 1, 3):
                    w_x(i, n).start()
                w_c(0, n).start()
            elif n - 4 < 4:
                for i in (1, 3, 2):
                    w_x(i, n - 4).wait_recv()
                    w_c(i, n - 4).start()
        for way in range(2):
            y_copy(step, way).wait_recv()
            if step < 4:
                y_copy(step + 1, way).start()
        if step == 3:

            @pl.when(jnp.logical_not(aligned))
            def _():
                for h in range(2):
                    half_send(h, 0).start()

    z_start(1)
    zc_copy(0).start()

    load_cos.wait()
    load_sin.wait()

    def turn(v):
        return v * cos_t[...] + pltpu.roll(v, 64, 1) * sin_t[...]

    def new_rows(z):
        return pl.ds(pl.multiple_of(PAST + z * 256, 256), 256)

    def q_dst():
        return qb.at[rows_z]

    def n_dst():
        return kvb.at[q, new_rows(zh)]

    def q_send(w, to):
        return remote(sres.at[w, 0], q_dst(), qs.at[w], qr.at[zh], to)

    def n_send(w, to):
        return remote(sres.at[w, 1], n_dst(), ns.at[w], nr.at[q, zh], to)

    def n_pass(kind, z):
        part = kvb.at[kind, new_rows(z)]
        return remote(part, part, nps.at[kind, z], nr.at[kind, z], sib)

    def project(w):
        out = jnp.dot(xg[...], wb[w], preferred_element_type=F32)
        part_q, part_n = out[:, :HEAD], out[:, HEAD:]
        sres[w, 0] = turn(part_q).astype(BF16)
        sres[w, 1] = jnp.where(q == 0, turn(part_n), part_n).astype(BF16)

    def spread_own(start):
        @pl.when(aligned)
        def _():
            if start:
                pltpu.make_async_copy(sres.at[0, 0], q_dst(), qr.at[zh]).start()
                pltpu.make_async_copy(sres.at[0, 1], n_dst(), nr.at[q, zh]).start()

        @pl.when(jnp.logical_not(aligned))
        def _():
            for copy in (q_send(0, dev(y=2 * j + c, c=q)), n_send(0, dev(y=2 * j + c))):
                copy.start() if start else copy.wait_send()

    def spread_other(start):
        to = functools.partial(dev, zh=1 - zh, y=2 * j + c)
        for copy in (q_send(1, to(c=q)), n_send(1, to())):
            copy.start() if start else copy.wait_send()

    for k in range(4):
        for i in (0, 1, 3, 2):
            w_c(i, k).wait_recv()
    project(1)
    spread_other(True)
    project(0)
    spread_own(True)

    @pl.when(jnp.logical_not(aligned))
    def _():
        for h in range(2):
            half_send(h, 1).start()

    m_s[...] = jnp.full(m_s.shape, NEG, F32)
    l_s[...] = jnp.zeros(l_s.shape, F32)
    acc_s[...] = jnp.zeros(acc_s.shape, F32)
    for z in range(2):
        arrived(qb.at[pl.ds(0, 256)], qr.at[z])
    z_arrived(1)
    z_start(2)
    zc_copy(1).start()
    zc_copy(7).start()
    arrived(cache_h, kfr.at[0])

    def attend(first, size, masked):
        keys = kvb[0, pl.ds(first, size), :]
        values = kvb[1, pl.ds(first, size), :]
        for tile in range(2):
            rows = pl.ds(tile * 256, 256)
            s = lax.dot_general(qb[rows, :], keys, (((1,), (1,)), ((), ())), preferred_element_type=F32)
            if masked:
                row = lax.broadcasted_iota(jnp.int32, s.shape, 0) + tile * 256
                col = lax.broadcasted_iota(jnp.int32, s.shape, 1)
                s = jnp.where(col <= row, s, NEG)
            old = m_s[rows, :]
            new = jnp.maximum(old, jnp.max(s, axis=1, keepdims=True))
            keep = jnp.exp2((old - new) * SCALE2)
            p = jnp.exp2((s - new[:, :1]) * SCALE2)
            l_s[rows, :] = l_s[rows, :] * keep + jnp.sum(p, axis=1, keepdims=True)
            acc_s[rows, :] = acc_s[rows, :] * keep + jnp.dot(p.astype(BF16), values, preferred_element_type=F32)
            m_s[rows, :] = new

    for k in range(2):
        arrived(kvb.at[0, pl.ds(0, 1024)], khr.at[k])
        half_pass(k).start()
        attend(pl.multiple_of(c * 2048 + k * 1024, 1024), 1024, False)
    z_arrived(2)
    z_start(3)
    zc_copy(2).start()
    zc_copy(6).start()

    @pl.when(aligned)
    def _():
        for kind in range(2):
            for z in range(2):
                arrived(kvb.at[0, pl.ds(0, 256)], nr.at[kind, z])
                n_pass(kind, z).start()

    for k in range(2):
        half_pass(k).wait_recv()
        attend(pl.multiple_of((1 - c) * 2048 + k * 1024, 1024), 1024, False)

    @pl.when(jnp.logical_not(aligned))
    def _():
        for kind in range(2):
            for z in range(2):
                arrived(kvb.at[0, pl.ds(0, 256)], nr.at[kind, z])

    attend(PAST, BLOCK, True)
    att[...] = (acc_s[...] / l_s[...]).astype(BF16)

    slot_x = own_rows(x)

    def a_copy(n, remotely):
        src = att.at[own_rows(n)]
        head = zh * 8 + 2 * j + c
        col = pl.multiple_of(head * HEAD, HEAD)
        dst = ar.at[slot_x, pl.ds(col, HEAD)]
        sem = ar_r.at[head]
        if remotely:
            return remote(src, dst, as_.at[n], sem, {"tensor": n, "dp": zl * 8 + x * 2 + q})
        return pltpu.make_async_copy(src, dst, sem)

    def a_start(n, carry):
        stays = jnp.logical_and(n == t, aligned)

        @pl.when(stays)
        def _():
            a_copy(n, False).start()

        @pl.when(jnp.logical_not(stays))
        def _():
            a_copy(n, True).start()

        return carry

    def a_sent(n, carry):
        @pl.when(jnp.logical_not(jnp.logical_and(n == t, aligned)))
        def _():
            a_copy(n, True).wait_send()

        return carry

    lax.fori_loop(0, 16, a_start, 0)
    z_arrived(3)
    z_start(4)
    zc_copy(3).start()
    zc_copy(5).start()

    def a_here(n, carry):
        arrived(ar.at[pl.ds(0, 32), pl.ds(0, HEAD)], ar_r.at[n])
        return carry

    lax.fori_loop(0, 16, a_here, 0)

    def ag(i):
        return remote(ar.at[slot_x], ar.at[slot_x], ags.at[i - 1], agr.at[i - 1], dev(x=(x + i) % 4))

    for i in (2, 1, 3):
        ag(i).start()
    z_arrived(4)
    zc_copy(4).start()
    for i in (1, 3, 2):
        ag(i).wait_recv()
    for i in range(8):
        zc_copy(i).wait_recv()

    def o_copy(i, k):
        n = (x + i) % 4
        dst = out_o.at[:, pl.ds(pl.multiple_of(x * 1024 + k * 512, 512), 512)]
        src = po.at[n, :, pl.ds(k * 512, 512)]
        if i == 0:
            return pltpu.make_async_copy(src, dst, ld.at[6 + k])
        return remote(src, dst, os_.at[i - 1, k], or_.at[i - 1, k], dev(x=n))

    for k in range(2):
        for n in (2 * k, 2 * k + 1):
            w = jnp.concatenate([wo[n, i].reshape(2048, HEAD) for i in range(2)], axis=1)
            out = jnp.dot(ar[...], w, preferred_element_type=F32).astype(BF16)
            for i in range(4):
                po[i, :, n * 256 : (n + 1) * 256] = out[i * 32 : (i + 1) * 32]
        for i in (2, 1, 3, 0):
            o_copy(i, k).start()
    for k in range(2):
        o_copy(0, k).wait()
        for i in (1, 3, 2):
            o_copy(i, k).wait_recv()

    for step in range(1, 5):
        for k in range(2):
            for way in range(2):
                if x_used(step, way, k):
                    x_copy(step, way, k).wait_send()
        for way in range(2):
            y_copy(step, way).wait_send()
            z_copy(step, way).wait_send()
    for k in range(4):
        w_z(k).wait_send()
        for i in range(4):
            w_c(i, k).wait_send()
            if i:
                w_x(i, k).wait_send()
    for i in range(8):
        zc_copy(i).wait_send()
    for k in range(2):
        half_pass(k).wait_send()
        for i in range(1, 4):
            o_copy(i, k).wait_send()
    for i in range(1, 4):
        ag(i).wait_send()

    @pl.when(aligned)
    def _():
        full_send().wait_send()
        for kind in range(2):
            for z in range(2):
                n_pass(kind, z).wait_send()

    @pl.when(jnp.logical_not(aligned))
    def _():
        for k in range(2):
            for h in range(2):
                half_send(h, k).wait_send()

    spread_own(False)
    spread_other(False)
    lax.fori_loop(0, 16, a_sent, 0)


def per_device(tokens, attn_gain, query_weight, key_value_weight, prefix_cache, out_weight, post_gain):
    cosine, sine = rope_tables()
    hbm = pl.BlockSpec(memory_space=pltpu.HBM)
    vmem = pl.BlockSpec(memory_space=pltpu.VMEM)
    dma = pltpu.SemaphoreType.DMA
    attn_sum = pl.pallas_call(
        kernel,
        out_shape=jax.ShapeDtypeStruct(tokens.shape, BF16),
        in_specs=[hbm, vmem, hbm, hbm, hbm, hbm, hbm, hbm],
        out_specs=vmem,
        scratch_shapes=[
            pltpu.VMEM((32, WIDTH), BF16),
            pltpu.VMEM((256, WIDTH), BF16),
            pltpu.VMEM((2, WIDTH, 256), BF16),
            pltpu.VMEM((256, HEAD), F32),
            pltpu.VMEM((256, HEAD), F32),
            pltpu.VMEM((2, 2, 256, HEAD), BF16),
            pltpu.VMEM((BLOCK, HEAD), BF16),
            pltpu.VMEM((2, PAST + BLOCK, HEAD), BF16),
            pltpu.VMEM((4, 2, 2, 8, HEAD, HEAD), BF16),
            pltpu.VMEM((BLOCK, HEAD), BF16),
            pltpu.VMEM((HEAD, 2048), BF16),
            pltpu.VMEM((4, 32, 1024), BF16),
            pltpu.VMEM((BLOCK, HEAD), F32),
            pltpu.VMEM((BLOCK, HEAD), F32),
            pltpu.VMEM((BLOCK, HEAD), F32),
            dma((8,)),
            dma((2, 4, 2)), dma((2, 4, 2)),
            dma((2, 4)), dma((2, 4)),
            dma((4,)), dma((4,)),
            dma((3, 4)), dma((3, 4)),
            dma((4, 4)), dma((4, 4)),
            dma((1,)), dma((1,)),
            dma((2, 2)), dma((2,)),
            dma((2,)), dma((2,)),
            dma((2,)), dma((2,)),
            dma((2,)), dma((2, 2)), dma((2, 2)),
            dma((2, 4)), dma((2, 4)),
            dma((8,)), dma((8,)),
            dma((16,)), dma((16,)),
            dma((3,)), dma((3,)),
            dma((3, 2)), dma((3, 2)),
        ],
        compiler_params=pltpu.CompilerParams(
            collective_id=0, has_side_effects=True, vmem_limit_bytes=60 * 2**20
        ),
        name="sublayer",
    )(
        tokens, attn_gain, query_weight, key_value_weight, prefix_cache,
        out_weight, jnp.asarray(cosine), jnp.asarray(sine),
    )
    residual_out = (tokens.astype(F32) + attn_sum.astype(F32)).astype(BF16)
    gain = post_gain.astype(F32)
    return residual_out, normed(residual_out.astype(F32), gain).astype(BF16)


def solution(mesh):
    rows = P(("dp", "tensor"), None)
    return jax.shard_map(
        per_device,
        mesh=mesh,
        in_specs=(rows, P(), P(None, "tensor"), P(None, "tensor"), P("dp", "tensor"), P("tensor", None), P()),
        out_specs=(rows, rows),
        check_vma=False,
    )
```

```python
import functools

import jax
import jax.numpy as jnp
import numpy as np
from jax import lax
from jax.experimental import pallas as pl
from jax.experimental.pallas import tpu as pltpu
from jax.sharding import PartitionSpec as P

MESH = pl.DeviceIdType.MESH
BF16 = jnp.bfloat16
F32 = jnp.float32
HEAD = 128
PAST = 4096
BLOCK = 512
WIDTH = 4096
BASE = 500000.0
EPS = 1e-05
SCALE2 = float(HEAD ** (-0.5) / np.log(2.0))
NEG = -1e30
Y_AT = (2, 4, 7)
Z_AT = (11, 13)


def rope_tables():
    positions = np.arange(PAST, PAST + BLOCK, dtype=np.float64)
    inverse = BASE ** (-np.arange(HEAD // 2, dtype=np.float64) * 2.0 / HEAD)
    angle = positions[:, None] * inverse[None, :]
    cosine = np.concatenate([np.cos(angle), np.cos(angle)], axis=1)
    sine = np.concatenate([-np.sin(angle), np.sin(angle)], axis=1)
    order = np.arange(BLOCK).reshape(2, 8, 2, 16).transpose(0, 2, 1, 3).reshape(-1)
    cosine, sine = cosine[order], sine[order]
    return cosine.astype(np.float32), sine.astype(np.float32)


def normed(rows, gain):
    mean_square = jnp.mean(rows * rows, axis=-1, keepdims=True)
    return rows * lax.rsqrt(mean_square + EPS) * gain


def kernel(
    tok_h, gain1_h, wq_h, wkv_h, cache_h, wout_h, gain2_h, cos_h, sin_h,
    out_o,
    tok, gain1, gain2, xg, wb, cos_t, sin_t, sres, qb, kvb, wo, att, ar, po, ob,
    m_s, l_s, acc_s,
    ld, xs, xr, ys, yr, wzs, wzr, wxs, wxr, wcs, wcr,
    kfs, kfr, khs, khr, kxs, kxr, qs, qr, ns, nr, nps,
    zs, zr, zcs, zcr, as_, ar_r, ags, agr, os_, or_,
):
    t = lax.axis_index("tensor")
    d = lax.axis_index("dp")
    zh, y = t // 8, t % 8
    zl, x, c = d // 8, (d // 2) % 4, d % 2
    j, q = y // 2, y % 2
    aligned = c == q
    zi = zh * 4 + zl

    def dev(zh=zh, y=y, zl=zl, x=x, c=c):
        return {"tensor": zh * 8 + y, "dp": zl * 8 + x * 2 + c}

    def remote(src, dst, ss, rs, to):
        return pltpu.make_async_remote_copy(
            src_ref=src, dst_ref=dst, send_sem=ss, recv_sem=rs,
            device_id=to, device_id_type=MESH,
        )

    def arrived(ref, sem):
        pltpu.make_async_copy(ref, ref, sem).wait()

    sib = dev(c=1 - c)
    up, down = dev(y=(y + 1) % 8), dev(y=(y + 7) % 8)

    def zdev(step):
        n = (zi + step) % 8
        return dev(zh=n // 4, zl=n % 4)

    load_tok = pltpu.make_async_copy(tok_h, tok, ld.at[0])
    load_wq = pltpu.make_async_copy(wq_h, wb.at[0, :, pl.ds(0, HEAD)], ld.at[1])
    load_wkv = pltpu.make_async_copy(wkv_h, wb.at[0, :, pl.ds(HEAD, HEAD)], ld.at[2])
    rows_z = pl.ds(pl.multiple_of(zh * 256, 256), 256)
    load_cos = pltpu.make_async_copy(cos_h.at[rows_z], cos_t, ld.at[3])
    load_sin = pltpu.make_async_copy(sin_h.at[rows_z], sin_t, ld.at[4])
    load_g1 = pltpu.make_async_copy(gain1_h, gain1, ld.at[6])
    load_g2 = pltpu.make_async_copy(gain2_h, gain2, ld.at[7])
    load_tok.start()
    load_g1.start()
    load_wq.start()
    load_wkv.start()

    def wo_piece(n):
        return wo.at[zl, c, zh, n]

    out_col = pl.multiple_of((x * 4 + zl) * 256 + c * HEAD, HEAD)
    load_wo = pltpu.make_async_copy(wout_h.at[:, pl.ds(out_col, HEAD)], wo_piece(y), ld.at[5])

    barrier = pltpu.get_barrier_semaphore()
    greeted = [up, down, zdev(1), zdev(7), sib, dev(y=2 * j + 1 - q, c=1 - c)]
    greeted += [dev(zh=1 - zh, zl=i) for i in range(4)]
    greeted += [dev(x=(x + i) % 4) for i in (1, 2, 3)]
    for to in greeted:
        pl.semaphore_signal(barrier, inc=1, device_id=to, device_id_type=MESH)
    load_wo.start()
    load_g2.start()
    load_cos.start()
    load_sin.start()

    load_tok.wait()

    load_g1.wait()
    gain = gain1[...].astype(F32).reshape(1, WIDTH)

    def half_of(n, k):
        return pl.ds(pl.multiple_of(k * 128 + n * 16, 16), 16)

    for k in range(2):
        xg[half_of(y, k), :] = normed(tok[pl.ds(k * 16, 16), :].astype(F32), gain).astype(BF16)
    load_wq.wait()
    load_wkv.wait()
    load_wo.wait()
    pl.semaphore_wait(barrier, len(greeted))

    def x_copy(step, way, k, h):
        n = (y - step + 1 + 8) % 8 if way == 0 else (y + step - 1) % 8
        part = xg.at[half_of(n, k), pl.ds(h * 2048, 2048)]
        at = (way, step - 1, k, h)
        return remote(part, part, xs.at[at], xr.at[at], up if way == 0 else down)

    def x_used(step, way, k):
        return step < 4 or way == k

    def y_copy(step, way):
        part = wo_piece((y - step + 1 + 8) % 8 if way == 0 else (y + step - 1) % 8)
        if step == 4:
            part = part.at[pl.ds(64 * way, 64)]
        return remote(part, part, ys.at[way, step - 1], yr.at[way, step - 1], up if way == 0 else down)

    for way in range(2):
        x_copy(1, way, 0, 0).start()
        y_copy(1, way).start()
    for k, h in ((0, 1), (1, 0), (1, 1)):
        for way in range(2):
            x_copy(1, way, k, h).start()

    def w_rows(xx, cc, k):
        return pl.ds(pl.multiple_of(xx * 1024 + cc * 512 + k * 128, 128), 128)

    def w_z(k):
        r = w_rows(x, c, zl)
        return remote(wb.at[0, r], wb.at[1, r], wzs.at[k], wzr.at[zl], dev(zh=1 - zh, zl=k))

    def w_x(way, k):
        r = w_rows(x, c, k)
        return remote(wb.at[1, r], wb.at[1, r], wxs.at[way, k], wxr.at[way, k], dev(x=(x + 1 + 2 * way) % 4))

    def w_far(k):
        way = k // 2
        r = w_rows((x + 3 + 2 * way) % 4, c, k)
        return remote(wb.at[1, r], wb.at[1, r], wxs.at[2, k], wxr.at[2, k], dev(x=(x + 1 + 2 * way) % 4))

    def w_c(i, k):
        r = w_rows((x + 4 - i) % 4, c, k)
        return remote(wb.at[1, r], wb.at[1, r], wcs.at[i, k], wcr.at[i, k], sib)

    for k in range(4):
        w_z(k).start()

    def full_local():
        return pltpu.make_async_copy(cache_h, kvb.at[q, pl.ds(0, PAST)], kfr.at[0])

    def full_send():
        return remote(cache_h, kvb.at[q, pl.ds(0, PAST)], kfs.at[0], kfr.at[0], sib)

    def half_rows(h, k):
        return pl.ds(pl.multiple_of(h * 2048 + k * 1024, 1024), 1024)

    def half_send(h, k):
        r = half_rows(h, k)
        return remote(cache_h.at[r], kvb.at[q, r], khs.at[h, k], khr.at[k], dev(y=2 * j + 1 - q, c=h))

    def half_pass(k):
        r = half_rows(c, k)
        return remote(kvb.at[1 - q, r], kvb.at[1 - q, r], kxs.at[k], kxr.at[k], sib)

    @pl.when(aligned)
    def _():
        full_local().start()
        full_send().start()

    def z_copy(step, way, k):
        n = (zi - step + 1 + 8) % 8 if way == 0 else (zi + step - 1) % 8
        part = wo.at[n % 4, c, n // 4, pl.ds(4 * k, 4)]
        return remote(part, part, zs.at[way, step - 1, k], zr.at[way, step - 1, k], zdev(1 if way == 0 else 7))

    def z_arrived(step, k):
        for way in range(2):
            if x_used(step, way, k):
                z_copy(step, way, k).wait_recv()

    def z_start(step, k):
        for way in range(2):
            if x_used(step, way, k):
                z_copy(step, way, k).start()

    def zc_copy(i):
        n = (zi + i) % 8
        part = wo.at[n % 4, c, n // 4]
        return remote(part, part, zcs.at[i], zcr.at[i], sib)

    def y_next(step):
        for way in range(2):
            y_copy(step, way).wait_recv()
            if step < 4:
                y_copy(step + 1, way).start()

    def z_next(step, k):
        z_arrived(step, k)
        z_start(step + 1, k)

    def z_share(step):
        zc_copy(step).start()
        zc_copy(8 - step).start()

    def weights_in():
        for n in range(4):
            arrived(wb.at[1, w_rows(x, c, n)], wzr.at[n])
            for way in range(2):
                w_x(way, n).start()
            w_c(0, n).start()

    def weights_on(n):
        for way in range(2):
            w_x(way, n).wait_recv()
            if way == n // 2:
                w_far(n).start()
            w_c(1 + 2 * way, n).start()

    def weights_far(n):
        w_far(n).wait_recv()
        w_c(2, n).start()

    def after(event):
        if event in Y_AT:
            y_next(Y_AT.index(event) + 2)
        if event == 5:
            weights_in()
        if event in (8, 9, 10, 11):
            weights_on(event - 8)
        if event == 11:

            @pl.when(jnp.logical_not(aligned))
            def _():
                for k in range(2):
                    for h in range(2):
                        half_send(h, k).start()

        if event in (12, 13, 14, 15):
            weights_far(event - 12)
        if event == Y_AT[2]:
            z_start(1, 0)
            z_start(1, 1)
            zc_copy(0).start()
        for k in range(2):
            if event == Z_AT[k]:
                z_next(1, k)
                if k == 1:
                    z_share(1)

    y_next(1)
    event = 0
    for step in range(1, 5):
        for k in range(2):
            for h in range(2):
                for way in range(2):
                    if x_used(step, way, k):
                        x_copy(step, way, k, h).wait_recv()
                        if step < 4 and x_used(step + 1, way, k):
                            x_copy(step + 1, way, k, h).start()
                after(event)
                event += 1

    load_cos.wait()
    load_sin.wait()

    def turn(v):
        return v * cos_t[...] + pltpu.roll(v, 64, 1) * sin_t[...]

    def new_rows(z):
        return pl.ds(pl.multiple_of(PAST + z * 256, 256), 256)

    def q_src(w, k):
        return sres.at[w, 0, pl.ds(k * 128, 128)]

    def q_dst(k):
        return qb.at[pl.ds(pl.multiple_of(k * 256 + zh * 128, 128), 128)]

    def n_dst():
        return kvb.at[q, new_rows(zh)]

    def q_send(w, k, to):
        return remote(q_src(w, k), q_dst(k), qs.at[w, k], qr.at[k, zh], to)

    def n_send(w, to):
        return remote(sres.at[w, 1], n_dst(), ns.at[w], nr.at[q, zh], to)

    def n_pass(kind, z):
        part = kvb.at[kind, new_rows(z)]
        return remote(part, part, nps.at[kind, z], nr.at[kind, z], sib)

    def project(w):
        out = jnp.dot(xg[...], wb[w], preferred_element_type=F32)
        part_q, part_n = out[:, :HEAD], out[:, HEAD:]
        sres[w, 0] = turn(part_q).astype(BF16)
        sres[w, 1] = jnp.where(q == 0, turn(part_n), part_n).astype(BF16)

    def spread_own(start):
        @pl.when(aligned)
        def _():
            if start:
                for k in range(2):
                    pltpu.make_async_copy(q_src(0, k), q_dst(k), qr.at[k, zh]).start()
                pltpu.make_async_copy(sres.at[0, 1], n_dst(), nr.at[q, zh]).start()

        @pl.when(jnp.logical_not(aligned))
        def _():
            to = functools.partial(dev, y=2 * j + c)
            for copy in (q_send(0, 0, to(c=q)), q_send(0, 1, to(c=q)), n_send(0, to())):
                copy.start() if start else copy.wait_send()

    def spread_other(start):
        to = functools.partial(dev, zh=1 - zh, y=2 * j + c)
        for copy in (q_send(1, 0, to(c=q)), q_send(1, 1, to(c=q)), n_send(1, to())):
            copy.start() if start else copy.wait_send()

    for k in range(4):
        for i in (0, 1, 3, 2):
            w_c(i, k).wait_recv()
    project(1)
    spread_other(True)
    project(0)
    spread_own(True)
    for k in range(2):
        z_next(2, k)
    z_share(2)

    m_s[...] = jnp.full(m_s.shape, NEG, F32)
    l_s[...] = jnp.zeros(l_s.shape, F32)
    acc_s[...] = jnp.zeros(acc_s.shape, F32)

    def q_arrived(g):
        for z in range(2):
            arrived(qb.at[pl.ds(0, 128)], qr.at[g, z])

    def attend(g, first, size, masked):
        keys = kvb[0, pl.ds(first, size), :]
        values = kvb[1, pl.ds(first, size), :]
        rows = pl.ds(g * 256, 256)
        s = lax.dot_general(qb[rows, :], keys, (((1,), (1,)), ((), ())), preferred_element_type=F32)
        if masked:
            n = lax.broadcasted_iota(jnp.int32, (256, 1), 0)
            query = (n // 128) * 256 + (n // 16) % 8 * 32 + g * 16 + n % 16
            n = lax.broadcasted_iota(jnp.int32, (1, size), 1)
            key = (n // 256) * 256 + (n // 16) % 8 * 32 + (n // 128) % 2 * 16 + n % 16
            s = jnp.where(key <= query, s, NEG)
        old = m_s[rows, :]
        new = jnp.maximum(old, jnp.max(s, axis=1, keepdims=True))
        keep = jnp.exp2((old - new) * SCALE2)
        p = jnp.exp2((s - new[:, :1]) * SCALE2)
        l_s[rows, :] = l_s[rows, :] * keep + jnp.sum(p, axis=1, keepdims=True)
        acc_s[rows, :] = acc_s[rows, :] * keep + jnp.dot(p.astype(BF16), values, preferred_element_type=F32)
        m_s[rows, :] = new

    def finish(g):
        rows = pl.ds(g * 256, 256)
        att[rows, :] = (acc_s[rows, :] / l_s[rows, :]).astype(BF16)

    def cached(h, k):
        return pl.multiple_of(h * 2048 + k * 1024, 1024)

    head = zh * 8 + 2 * j + c
    col = pl.ds(pl.multiple_of(head * HEAD, HEAD), HEAD)
    slot_x = pl.ds(pl.multiple_of(x * 16, 16), 16)

    def a_stays(n):
        return jnp.logical_and(n == t, aligned)

    def a_copy(g, n, remotely):
        src = att.at[pl.ds(g * 256 + n * 16, 16)]
        dst = ar.at[g, slot_x, col]
        sem = ar_r.at[g, head]
        if remotely:
            return remote(src, dst, as_.at[g, n], sem, {"tensor": n, "dp": zl * 8 + x * 2 + q})
        return pltpu.make_async_copy(src, dst, sem)

    def a_start(g):
        for n in range(16):

            @pl.when(a_stays(n))
            def _():
                a_copy(g, n, False).start()

            @pl.when(jnp.logical_not(a_stays(n)))
            def _():
                a_copy(g, n, True).start()

    def a_sent(g):
        for n in range(16):

            @pl.when(jnp.logical_not(a_stays(n)))
            def _():
                a_copy(g, n, True).wait_send()

    def a_arrived(g):
        for n in range(16):
            arrived(ar.at[g, pl.ds(0, 16), pl.ds(0, HEAD)], ar_r.at[g, n])

    def ag(g, i):
        part = ar.at[g, slot_x]
        return remote(part, part, ags.at[g, i - 1], agr.at[g, i - 1], dev(x=(x + i) % 4))

    def o_copy(g, i):
        n = (x + i) % 4
        dst = ob.at[pl.ds(g * 16, 16), pl.ds(pl.multiple_of(x * 1024, 1024), 1024)]
        if i == 0:
            return pltpu.make_async_copy(po.at[g, n], dst, ld.at[8 + g])
        return remote(po.at[g, n], dst, os_.at[g, i - 1], or_.at[g, i - 1], dev(x=n))

    def product(g):
        for n in range(4):
            w = jnp.concatenate([wo[n, i].reshape(2048, HEAD) for i in range(2)], axis=1)
            out = jnp.dot(ar[g], w, preferred_element_type=F32).astype(BF16)
            for i in range(4):
                po[g, i, :, n * 256 : (n + 1) * 256] = out[i * 16 : (i + 1) * 16]
        for i in (2, 1, 3, 0):
            o_copy(g, i).start()

    def output(g):
        o_copy(g, 0).wait()
        for i in (1, 3, 2):
            o_copy(g, i).wait_recv()
        rows = pl.ds(g * 16, 16)
        res = (tok[rows, :].astype(F32) + ob[rows, :].astype(F32)).astype(BF16)
        out_o[0, rows, :] = res
        out_o[1, rows, :] = normed(res.astype(F32), gain2[...].astype(F32).reshape(1, WIDTH)).astype(BF16)

    q_arrived(0)
    arrived(cache_h, kfr.at[0])
    for k in range(2):
        arrived(kvb.at[0, pl.ds(0, 1024)], khr.at[k])
        half_pass(k).start()
        attend(0, cached(c, k), 1024, False)
    @pl.when(aligned)
    def _():
        for kind in range(2):
            for z in range(2):
                arrived(kvb.at[0, pl.ds(0, 256)], nr.at[kind, z])
                n_pass(kind, z).start()

    for k in range(2):
        half_pass(k).wait_recv()
        attend(0, cached(1 - c, k), 1024, False)

    @pl.when(jnp.logical_not(aligned))
    def _():
        for kind in range(2):
            for z in range(2):
                arrived(kvb.at[0, pl.ds(0, 256)], nr.at[kind, z])

    attend(0, PAST, BLOCK, True)
    finish(0)
    a_start(0)
    q_arrived(1)
    for n in range(4):
        attend(1, n * 1024, 1024, False)
        if n == 1:
            for k in range(2):
                z_next(3, k)
            z_share(3)
    attend(1, PAST, BLOCK, True)
    finish(1)
    a_start(1)
    for g in range(2):
        a_arrived(g)
        for i in (2, 1, 3):
            ag(g, i).start()
    for k in range(2):
        z_arrived(4, k)
    zc_copy(4).start()
    for i in range(8):
        zc_copy(i).wait_recv()
    load_g2.wait()
    for g in range(2):
        for i in (1, 3, 2):
            ag(g, i).wait_recv()
        product(g)
    for g in range(2):
        output(g)

    for step in range(1, 5):
        for k in range(2):
            for way in range(2):
                if x_used(step, way, k):
                    for h in range(2):
                        x_copy(step, way, k, h).wait_send()
                    z_copy(step, way, k).wait_send()
        for way in range(2):
            y_copy(step, way).wait_send()
    for k in range(4):
        w_z(k).wait_send()
        for i in range(4):
            w_c(i, k).wait_send()
        for way in range(2):
            w_x(way, k).wait_send()
        w_far(k).wait_send()
    for i in range(8):
        zc_copy(i).wait_send()
    for k in range(2):
        half_pass(k).wait_send()
        a_sent(k)
        for i in range(1, 4):
            o_copy(k, i).wait_send()
            ag(k, i).wait_send()

    @pl.when(aligned)
    def _():
        full_send().wait_send()
        for kind in range(2):
            for z in range(2):
                n_pass(kind, z).wait_send()

    @pl.when(jnp.logical_not(aligned))
    def _():
        for k in range(2):
            for h in range(2):
                half_send(h, k).wait_send()

    spread_own(False)
    spread_other(False)


def per_device(tokens, attn_gain, query_weight, key_value_weight, prefix_cache, out_weight, post_gain):
    cosine, sine = rope_tables()
    hbm = pl.BlockSpec(memory_space=pltpu.HBM)
    vmem = pl.BlockSpec(memory_space=pltpu.VMEM)
    dma = pltpu.SemaphoreType.DMA
    rows = jax.ShapeDtypeStruct((2, *tokens.shape), BF16)
    out = pl.pallas_call(
        kernel,
        out_shape=rows,
        in_specs=[hbm] * 9,
        out_specs=vmem,
        scratch_shapes=[
            pltpu.VMEM((32, WIDTH), BF16),
            pltpu.VMEM((WIDTH,), BF16),
            pltpu.VMEM((WIDTH,), BF16),
            pltpu.VMEM((256, WIDTH), BF16),
            pltpu.VMEM((2, WIDTH, 256), BF16),
            pltpu.VMEM((256, HEAD), F32),
            pltpu.VMEM((256, HEAD), F32),
            pltpu.VMEM((2, 2, 256, HEAD), BF16),
            pltpu.VMEM((BLOCK, HEAD), BF16),
            pltpu.VMEM((2, PAST + BLOCK, HEAD), BF16),
            pltpu.VMEM((4, 2, 2, 8, HEAD, HEAD), BF16),
            pltpu.VMEM((BLOCK, HEAD), BF16),
            pltpu.VMEM((2, 64, 2048), BF16),
            pltpu.VMEM((2, 4, 16, 1024), BF16),
            pltpu.VMEM((32, WIDTH), BF16),
            pltpu.VMEM((BLOCK, HEAD), F32),
            pltpu.VMEM((BLOCK, HEAD), F32),
            pltpu.VMEM((BLOCK, HEAD), F32),
            dma((10,)),
            dma((2, 4, 2, 2)), dma((2, 4, 2, 2)),
            dma((2, 4)), dma((2, 4)),
            dma((4,)), dma((4,)),
            dma((3, 4)), dma((3, 4)),
            dma((4, 4)), dma((4, 4)),
            dma((1,)), dma((1,)),
            dma((2, 2)), dma((2,)),
            dma((2,)), dma((2,)),
            dma((2, 2)), dma((2, 2)),
            dma((2,)), dma((2, 2)), dma((2, 2)),
            dma((2, 4, 2)), dma((2, 4, 2)),
            dma((8,)), dma((8,)),
            dma((2, 16)), dma((2, 16)),
            dma((2, 3)), dma((2, 3)),
            dma((2, 3)), dma((2, 3)),
        ],
        compiler_params=pltpu.CompilerParams(
            collective_id=0, has_side_effects=True, vmem_limit_bytes=60 * 2**20
        ),
        name="sublayer",
    )(
        tokens, attn_gain, query_weight, key_value_weight, prefix_cache,
        out_weight, post_gain, jnp.asarray(cosine), jnp.asarray(sine),
    )
    return out[0], out[1]

def solution(mesh):
    rows = P(("dp", "tensor"), None)
    return jax.shard_map(
        per_device,
        mesh=mesh,
        in_specs=(rows, P(), P(None, "tensor"), P(None, "tensor"), P("dp", "tensor"), P("tensor", None), P()),
        out_specs=(rows, rows),
        check_vma=False,
    )
```

```python
import functools

import jax
import jax.numpy as jnp
import numpy as np
from jax import lax
from jax.experimental import pallas as pl
from jax.experimental.pallas import tpu as pltpu
from jax.sharding import PartitionSpec as P

MESH = pl.DeviceIdType.MESH
BF16 = jnp.bfloat16
F32 = jnp.float32
HEAD = 128
PAST = 4096
BLOCK = 512
WIDTH = 4096
BASE = 500000.0
EPS = 1e-05
SCALE2 = float(HEAD ** (-0.5) / np.log(2.0))
NEG = -1e30
Y_AT = (2, 4, 7)
Z_AT = (11, 13)


def rope_tables():
    positions = np.arange(PAST, PAST + BLOCK, dtype=np.float64)
    inverse = BASE ** (-np.arange(HEAD // 2, dtype=np.float64) * 2.0 / HEAD)
    angle = positions[:, None] * inverse[None, :]
    cosine = np.concatenate([np.cos(angle), np.cos(angle)], axis=1)
    sine = np.concatenate([-np.sin(angle), np.sin(angle)], axis=1)
    order = np.arange(BLOCK).reshape(2, 8, 2, 16).transpose(0, 2, 1, 3).reshape(-1)
    cosine, sine = cosine[order], sine[order]
    return cosine.astype(np.float32), sine.astype(np.float32)


def normed(rows, gain):
    mean_square = jnp.mean(rows * rows, axis=-1, keepdims=True)
    return rows * lax.rsqrt(mean_square + EPS) * gain


def kernel(
    tok_h, gain1_h, wq_h, wkv_h, cache_h, wout_h, gain2_h, cos_h, sin_h,
    out_o,
    tok, gain1, gain2, xg, wb, cos_t, sin_t, sres, qb, kvb, wo, att, ar, po, ob,
    m_s, l_s, acc_s,
    ld, xs, xr, ys, yr, wzs, wzr, wxs, wxr, wcs, wcr,
    kfs, kfr, khs, khr, kxs, kxr, qs, qr, ns, nr, nps,
    zs, zr, zcs, zcr, as_, ar_r, ags, agr, os_, or_,
):
    t = lax.axis_index("tensor")
    d = lax.axis_index("dp")
    zh, y = t // 8, t % 8
    zl, x, c = d // 8, (d // 2) % 4, d % 2
    j, q = y // 2, y % 2
    aligned = c == q
    zi = zh * 4 + zl

    def dev(zh=zh, y=y, zl=zl, x=x, c=c):
        return {"tensor": zh * 8 + y, "dp": zl * 8 + x * 2 + c}

    def remote(src, dst, ss, rs, to):
        return pltpu.make_async_remote_copy(
            src_ref=src, dst_ref=dst, send_sem=ss, recv_sem=rs,
            device_id=to, device_id_type=MESH,
        )

    def arrived(ref, sem):
        pltpu.make_async_copy(ref, ref, sem).wait()

    sib = dev(c=1 - c)
    up, down = dev(y=(y + 1) % 8), dev(y=(y + 7) % 8)

    def zdev(step):
        n = (zi + step) % 8
        return dev(zh=n // 4, zl=n % 4)

    load_tok = pltpu.make_async_copy(tok_h, tok, ld.at[0])
    load_wq = pltpu.make_async_copy(wq_h, wb.at[0, :, pl.ds(0, HEAD)], ld.at[1])
    load_wkv = pltpu.make_async_copy(wkv_h, wb.at[0, :, pl.ds(HEAD, HEAD)], ld.at[2])
    rows_z = pl.ds(pl.multiple_of(zh * 256, 256), 256)
    load_cos = pltpu.make_async_copy(cos_h.at[rows_z], cos_t, ld.at[3])
    load_sin = pltpu.make_async_copy(sin_h.at[rows_z], sin_t, ld.at[4])
    load_g1 = pltpu.make_async_copy(gain1_h, gain1, ld.at[6])
    load_g2 = pltpu.make_async_copy(gain2_h, gain2, ld.at[7])
    load_tok.start()
    load_g1.start()
    load_wq.start()
    load_wkv.start()

    def wo_piece(n):
        return wo.at[zl, c, zh, n]

    out_col = pl.multiple_of((x * 4 + zl) * 256 + c * HEAD, HEAD)
    load_wo = pltpu.make_async_copy(wout_h.at[:, pl.ds(out_col, HEAD)], wo_piece(y), ld.at[5])

    barrier = pltpu.get_barrier_semaphore()
    greeted = [up, down, zdev(1), zdev(7), sib, dev(y=2 * j + 1 - q, c=1 - c)]
    greeted += [dev(zh=1 - zh, zl=i) for i in range(4)]
    greeted += [dev(x=(x + i) % 4) for i in (1, 2, 3)]
    for to in greeted:
        pl.semaphore_signal(barrier, inc=1, device_id=to, device_id_type=MESH)
    load_wo.start()
    load_g2.start()
    load_cos.start()
    load_sin.start()

    load_tok.wait()

    load_g1.wait()
    gain = gain1[...].astype(F32).reshape(1, WIDTH)

    def half_of(n, k):
        return pl.ds(pl.multiple_of(k * 128 + n * 16, 16), 16)

    for k in range(2):
        xg[half_of(y, k), :] = normed(tok[pl.ds(k * 16, 16), :].astype(F32), gain).astype(BF16)
    load_wq.wait()
    load_wkv.wait()
    load_wo.wait()
    pl.semaphore_wait(barrier, len(greeted))

    def x_copy(step, way, k, h):
        n = (y - step + 1 + 8) % 8 if way == 0 else (y + step - 1) % 8
        part = xg.at[half_of(n, k), pl.ds(h * 2048, 2048)]
        at = (way, step - 1, k, h)
        return remote(part, part, xs.at[at], xr.at[at], up if way == 0 else down)

    def x_used(step, way, k):
        return step < 4 or way == k

    def y_copy(step, way):
        part = wo_piece((y - step + 1 + 8) % 8 if way == 0 else (y + step - 1) % 8)
        if step == 4:
            part = part.at[pl.ds(64 * way, 64)]
        return remote(part, part, ys.at[way, step - 1], yr.at[way, step - 1], up if way == 0 else down)

    for way in range(2):
        x_copy(1, way, 0, 0).start()
        y_copy(1, way).start()
    for k, h in ((0, 1), (1, 0), (1, 1)):
        for way in range(2):
            x_copy(1, way, k, h).start()

    def w_rows(xx, cc, k):
        return pl.ds(pl.multiple_of(xx * 1024 + cc * 512 + k * 128, 128), 128)

    def w_z(k):
        r = w_rows(x, c, zl)
        return remote(wb.at[0, r], wb.at[1, r], wzs.at[k], wzr.at[zl], dev(zh=1 - zh, zl=k))

    def w_x(way, k):
        r = w_rows(x, c, k)
        return remote(wb.at[1, r], wb.at[1, r], wxs.at[way, k], wxr.at[way, k], dev(x=(x + 1 + 2 * way) % 4))

    def w_far(k):
        way = k // 2
        r = w_rows((x + 3 + 2 * way) % 4, c, k)
        return remote(wb.at[1, r], wb.at[1, r], wxs.at[2, k], wxr.at[2, k], dev(x=(x + 1 + 2 * way) % 4))

    def w_c(i, k):
        r = w_rows((x + 4 - i) % 4, c, k)
        return remote(wb.at[1, r], wb.at[1, r], wcs.at[i, k], wcr.at[i, k], sib)

    for k in range(4):
        w_z(k).start()

    def full_local():
        return pltpu.make_async_copy(cache_h, kvb.at[q, pl.ds(0, PAST)], kfr.at[0])

    def full_send():
        return remote(cache_h, kvb.at[q, pl.ds(0, PAST)], kfs.at[0], kfr.at[0], sib)

    def half_rows(h, k):
        return pl.ds(pl.multiple_of(h * 2048 + k * 1024, 1024), 1024)

    def half_send(h, k):
        r = half_rows(h, k)
        return remote(cache_h.at[r], kvb.at[q, r], khs.at[h, k], khr.at[k], dev(y=2 * j + 1 - q, c=h))

    def half_pass(k):
        r = half_rows(c, k)
        return remote(kvb.at[1 - q, r], kvb.at[1 - q, r], kxs.at[k], kxr.at[k], sib)

    @pl.when(aligned)
    def _():
        full_local().start()
        full_send().start()

    def z_copy(step, way, k):
        n = (zi - step + 1 + 8) % 8 if way == 0 else (zi + step - 1) % 8
        part = wo.at[n % 4, c, n // 4, pl.ds(4 * k, 4)]
        return remote(part, part, zs.at[way, step - 1, k], zr.at[way, step - 1, k], zdev(1 if way == 0 else 7))

    def z_arrived(step, k):
        for way in range(2):
            if x_used(step, way, k):
                z_copy(step, way, k).wait_recv()

    def z_start(step, k):
        for way in range(2):
            if x_used(step, way, k):
                z_copy(step, way, k).start()

    def zc_copy(i):
        n = (zi + i) % 8
        part = wo.at[n % 4, c, n // 4]
        return remote(part, part, zcs.at[i], zcr.at[i], sib)

    def y_next(step):
        for way in range(2):
            y_copy(step, way).wait_recv()
            if step < 4:
                y_copy(step + 1, way).start()

    def z_next(step, k):
        z_arrived(step, k)
        z_start(step + 1, k)

    def z_share(step):
        zc_copy(step).start()
        zc_copy(8 - step).start()

    def weights_in():
        for n in range(4):
            arrived(wb.at[1, w_rows(x, c, n)], wzr.at[n])
            for way in range(2):
                w_x(way, n).start()
            w_c(0, n).start()

    def weights_on(n):
        for way in range(2):
            w_x(way, n).wait_recv()
            if way == n // 2:
                w_far(n).start()
            w_c(1 + 2 * way, n).start()

    def weights_far(n):
        w_far(n).wait_recv()
        w_c(2, n).start()

    def after(event):
        if event in Y_AT:
            y_next(Y_AT.index(event) + 2)
        if event == 5:
            weights_in()
        if event in (8, 9, 10, 11):
            weights_on(event - 8)
        if event in (11, 15):

            @pl.when(jnp.logical_not(aligned))
            def _():
                for h in range(2):
                    half_send(h, (event - 11) // 4).start()

        if event in (12, 13, 14, 15):
            weights_far(event - 12)
        if event == Y_AT[2]:
            z_start(1, 0)
            z_start(1, 1)
            zc_copy(0).start()
        for k in range(2):
            if event == Z_AT[k]:
                z_next(1, k)
                if k == 1:
                    z_share(1)

    y_next(1)
    event = 0
    for step in range(1, 5):
        for k in range(2):
            for h in range(2):
                for way in range(2):
                    if x_used(step, way, k):
                        x_copy(step, way, k, h).wait_recv()
                        if step < 4 and x_used(step + 1, way, k):
                            x_copy(step + 1, way, k, h).start()
                after(event)
                event += 1

    load_cos.wait()
    load_sin.wait()

    def turn(v):
        return v * cos_t[...] + pltpu.roll(v, 64, 1) * sin_t[...]

    def new_rows(z):
        return pl.ds(pl.multiple_of(PAST + z * 256, 256), 256)

    def q_src(w, k):
        return sres.at[w, 0, pl.ds(k * 128, 128)]

    def q_dst(k):
        return qb.at[pl.ds(pl.multiple_of(k * 256 + zh * 128, 128), 128)]

    def n_dst():
        return kvb.at[q, new_rows(zh)]

    def q_send(w, k, to):
        return remote(q_src(w, k), q_dst(k), qs.at[w, k], qr.at[k, zh], to)

    def n_send(w, to):
        return remote(sres.at[w, 1], n_dst(), ns.at[w], nr.at[q, zh], to)

    def n_pass(kind, z):
        part = kvb.at[kind, new_rows(z)]
        return remote(part, part, nps.at[kind, z], nr.at[kind, z], sib)

    def project(w):
        out = jnp.dot(xg[...], wb[w], preferred_element_type=F32)
        part_q, part_n = out[:, :HEAD], out[:, HEAD:]
        sres[w, 0] = turn(part_q).astype(BF16)
        sres[w, 1] = jnp.where(q == 0, turn(part_n), part_n).astype(BF16)

    def spread_own(start):
        @pl.when(aligned)
        def _():
            if start:
                for k in range(2):
                    pltpu.make_async_copy(q_src(0, k), q_dst(k), qr.at[k, zh]).start()
                pltpu.make_async_copy(sres.at[0, 1], n_dst(), nr.at[q, zh]).start()

        @pl.when(jnp.logical_not(aligned))
        def _():
            to = functools.partial(dev, y=2 * j + c)
            for copy in (q_send(0, 0, to(c=q)), q_send(0, 1, to(c=q)), n_send(0, to())):
                copy.start() if start else copy.wait_send()

    def spread_other(start):
        to = functools.partial(dev, zh=1 - zh, y=2 * j + c)
        for copy in (q_send(1, 0, to(c=q)), q_send(1, 1, to(c=q)), n_send(1, to())):
            copy.start() if start else copy.wait_send()

    for k in range(4):
        for i in (0, 1, 3, 2):
            w_c(i, k).wait_recv()
    project(1)
    spread_other(True)
    project(0)
    spread_own(True)
    for k in range(2):
        z_next(2, k)
    z_share(2)

    m_s[...] = jnp.full(m_s.shape, NEG, F32)
    l_s[...] = jnp.zeros(l_s.shape, F32)
    acc_s[...] = jnp.zeros(acc_s.shape, F32)

    def q_arrived(g):
        for z in range(2):
            arrived(qb.at[pl.ds(0, 128)], qr.at[g, z])

    def attend(g, first, size, masked):
        keys = kvb[0, pl.ds(first, size), :]
        values = kvb[1, pl.ds(first, size), :]
        rows = pl.ds(g * 256, 256)
        s = lax.dot_general(qb[rows, :], keys, (((1,), (1,)), ((), ())), preferred_element_type=F32)
        if masked:
            n = lax.broadcasted_iota(jnp.int32, (256, 1), 0)
            query = (n // 128) * 256 + (n // 16) % 8 * 32 + g * 16 + n % 16
            n = lax.broadcasted_iota(jnp.int32, (1, size), 1)
            key = (n // 256) * 256 + (n // 16) % 8 * 32 + (n // 128) % 2 * 16 + n % 16
            s = jnp.where(key <= query, s, NEG)
        old = m_s[rows, :]
        new = jnp.maximum(old, jnp.max(s, axis=1, keepdims=True))
        keep = jnp.exp2((old - new) * SCALE2)
        p = jnp.exp2((s - new[:, :1]) * SCALE2)
        l_s[rows, :] = l_s[rows, :] * keep + jnp.sum(p, axis=1, keepdims=True)
        acc_s[rows, :] = acc_s[rows, :] * keep + jnp.dot(p.astype(BF16), values, preferred_element_type=F32)
        m_s[rows, :] = new

    def finish(g):
        rows = pl.ds(g * 256, 256)
        att[rows, :] = (acc_s[rows, :] / l_s[rows, :]).astype(BF16)

    def cached(h, k):
        return pl.multiple_of(h * 2048 + k * 1024, 1024)

    head = zh * 8 + 2 * j + c
    col = pl.ds(pl.multiple_of(head * HEAD, HEAD), HEAD)
    slot_x = pl.ds(pl.multiple_of(x * 16, 16), 16)

    def a_stays(n):
        return jnp.logical_and(n == t, aligned)

    def a_copy(g, n, remotely):
        src = att.at[pl.ds(g * 256 + n * 16, 16)]
        dst = ar.at[g, slot_x, col]
        sem = ar_r.at[g, head]
        if remotely:
            return remote(src, dst, as_.at[g, n], sem, {"tensor": n, "dp": zl * 8 + x * 2 + q})
        return pltpu.make_async_copy(src, dst, sem)

    def a_start(g):
        for n in range(16):

            @pl.when(a_stays(n))
            def _():
                a_copy(g, n, False).start()

            @pl.when(jnp.logical_not(a_stays(n)))
            def _():
                a_copy(g, n, True).start()

    def a_sent(g):
        for n in range(16):

            @pl.when(jnp.logical_not(a_stays(n)))
            def _():
                a_copy(g, n, True).wait_send()

    def a_arrived(g):
        for n in range(16):
            arrived(ar.at[g, pl.ds(0, 16), pl.ds(0, HEAD)], ar_r.at[g, n])

    def ag(g, i):
        part = ar.at[g, slot_x]
        return remote(part, part, ags.at[g, i - 1], agr.at[g, i - 1], dev(x=(x + i) % 4))

    def o_copy(g, i):
        n = (x + i) % 4
        dst = ob.at[pl.ds(g * 16, 16), pl.ds(pl.multiple_of(x * 1024, 1024), 1024)]
        if i == 0:
            return pltpu.make_async_copy(po.at[g, n], dst, ld.at[8 + g])
        return remote(po.at[g, n], dst, os_.at[g, i - 1], or_.at[g, i - 1], dev(x=n))

    def product(g):
        for n in range(4):
            w = jnp.concatenate([wo[n, i].reshape(2048, HEAD) for i in range(2)], axis=1)
            out = jnp.dot(ar[g], w, preferred_element_type=F32).astype(BF16)
            for i in range(4):
                po[g, i, :, n * 256 : (n + 1) * 256] = out[i * 16 : (i + 1) * 16]
        for i in (2, 1, 3, 0):
            o_copy(g, i).start()

    def output(g):
        o_copy(g, 0).wait()
        for i in (1, 3, 2):
            o_copy(g, i).wait_recv()
        rows = pl.ds(g * 16, 16)
        res = (tok[rows, :].astype(F32) + ob[rows, :].astype(F32)).astype(BF16)
        out_o[0, rows, :] = res
        out_o[1, rows, :] = normed(res.astype(F32), gain2[...].astype(F32).reshape(1, WIDTH)).astype(BF16)

    q_arrived(0)
    arrived(cache_h, kfr.at[0])
    for k in range(2):
        arrived(kvb.at[0, pl.ds(0, 1024)], khr.at[k])
        half_pass(k).start()
        attend(0, cached(c, k), 1024, False)
    @pl.when(aligned)
    def _():
        for kind in range(2):
            for z in range(2):
                arrived(kvb.at[0, pl.ds(0, 256)], nr.at[kind, z])
                n_pass(kind, z).start()

    for k in range(2):
        half_pass(k).wait_recv()
        attend(0, cached(1 - c, k), 1024, False)

    @pl.when(jnp.logical_not(aligned))
    def _():
        for kind in range(2):
            for z in range(2):
                arrived(kvb.at[0, pl.ds(0, 256)], nr.at[kind, z])

    attend(0, PAST, BLOCK, True)
    finish(0)
    a_start(0)
    q_arrived(1)
    for n in range(4):
        attend(1, n * 1024, 1024, False)
        if n == 0:
            for k in range(2):
                z_next(3, k)
            z_share(3)
    attend(1, PAST, BLOCK, True)
    finish(1)
    a_start(1)
    for g in range(2):
        a_arrived(g)
        for i in (2, 1, 3):
            ag(g, i).start()
    for k in range(2):
        z_arrived(4, k)
    zc_copy(4).start()
    for i in range(8):
        zc_copy(i).wait_recv()
    load_g2.wait()
    for g in range(2):
        for i in (1, 3, 2):
            ag(g, i).wait_recv()
        product(g)
    for g in range(2):
        output(g)

    for step in range(1, 5):
        for k in range(2):
            for way in range(2):
                if x_used(step, way, k):
                    for h in range(2):
                        x_copy(step, way, k, h).wait_send()
                    z_copy(step, way, k).wait_send()
        for way in range(2):
            y_copy(step, way).wait_send()
    for k in range(4):
        w_z(k).wait_send()
        for i in range(4):
            w_c(i, k).wait_send()
        for way in range(2):
            w_x(way, k).wait_send()
        w_far(k).wait_send()
    for i in range(8):
        zc_copy(i).wait_send()
    for k in range(2):
        half_pass(k).wait_send()
        a_sent(k)
        for i in range(1, 4):
            o_copy(k, i).wait_send()
            ag(k, i).wait_send()

    @pl.when(aligned)
    def _():
        full_send().wait_send()
        for kind in range(2):
            for z in range(2):
                n_pass(kind, z).wait_send()

    @pl.when(jnp.logical_not(aligned))
    def _():
        for k in range(2):
            for h in range(2):
                half_send(h, k).wait_send()

    spread_own(False)
    spread_other(False)


def per_device(tokens, attn_gain, query_weight, key_value_weight, prefix_cache, out_weight, post_gain):
    cosine, sine = rope_tables()
    hbm = pl.BlockSpec(memory_space=pltpu.HBM)
    vmem = pl.BlockSpec(memory_space=pltpu.VMEM)
    dma = pltpu.SemaphoreType.DMA
    rows = jax.ShapeDtypeStruct((2, *tokens.shape), BF16)
    out = pl.pallas_call(
        kernel,
        out_shape=rows,
        in_specs=[hbm] * 9,
        out_specs=vmem,
        scratch_shapes=[
            pltpu.VMEM((32, WIDTH), BF16),
            pltpu.VMEM((WIDTH,), BF16),
            pltpu.VMEM((WIDTH,), BF16),
            pltpu.VMEM((256, WIDTH), BF16),
            pltpu.VMEM((2, WIDTH, 256), BF16),
            pltpu.VMEM((256, HEAD), F32),
            pltpu.VMEM((256, HEAD), F32),
            pltpu.VMEM((2, 2, 256, HEAD), BF16),
            pltpu.VMEM((BLOCK, HEAD), BF16),
            pltpu.VMEM((2, PAST + BLOCK, HEAD), BF16),
            pltpu.VMEM((4, 2, 2, 8, HEAD, HEAD), BF16),
            pltpu.VMEM((BLOCK, HEAD), BF16),
            pltpu.VMEM((2, 64, 2048), BF16),
            pltpu.VMEM((2, 4, 16, 1024), BF16),
            pltpu.VMEM((32, WIDTH), BF16),
            pltpu.VMEM((BLOCK, HEAD), F32),
            pltpu.VMEM((BLOCK, HEAD), F32),
            pltpu.VMEM((BLOCK, HEAD), F32),
            dma((10,)),
            dma((2, 4, 2, 2)), dma((2, 4, 2, 2)),
            dma((2, 4)), dma((2, 4)),
            dma((4,)), dma((4,)),
            dma((3, 4)), dma((3, 4)),
            dma((4, 4)), dma((4, 4)),
            dma((1,)), dma((1,)),
            dma((2, 2)), dma((2,)),
            dma((2,)), dma((2,)),
            dma((2, 2)), dma((2, 2)),
            dma((2,)), dma((2, 2)), dma((2, 2)),
            dma((2, 4, 2)), dma((2, 4, 2)),
            dma((8,)), dma((8,)),
            dma((2, 16)), dma((2, 16)),
            dma((2, 3)), dma((2, 3)),
            dma((2, 3)), dma((2, 3)),
        ],
        compiler_params=pltpu.CompilerParams(
            collective_id=0, has_side_effects=True, vmem_limit_bytes=60 * 2**20
        ),
        name="sublayer",
    )(
        tokens, attn_gain, query_weight, key_value_weight, prefix_cache,
        out_weight, post_gain, jnp.asarray(cosine), jnp.asarray(sine),
    )
    return out[0], out[1]

def solution(mesh):
    rows = P(("dp", "tensor"), None)
    return jax.shard_map(
        per_device,
        mesh=mesh,
        in_specs=(rows, P(), P(None, "tensor"), P(None, "tensor"), P("dp", "tensor"), P("tensor", None), P()),
        out_specs=(rows, rows),
        check_vma=False,
    )
```
